256 devices in a mesh: row: 64 (over y, z, core), col: 4 (over x).
Axes of the slice: x: 4, y: 4, z: 8, core: 2. Of those that a mesh axis runs over, the one named last changes fastest.
Arguments:
- right_side: float32 [3, 65536, 512], P(None, 'row', 'col'), may hold values from -48 to 48
- onsite: float32 [65536], P('row'), may hold values from 8 to 16
- energies: float32 [512], P('col'), may hold values from -1 to -0.25
- ks_tiles: bfloat16 [512, 24, 128, 128], P('row'), may hold values from -1 to 1
- correlation_tiles: bfloat16 [512, 8, 128, 128], P('row'), may hold values from -0.1875 to 0.1875
- tile_slot: int32 [512, 24], P('row'), may hold values from 0 to 27, as said below
- readers: int32 [64, 7, 4], P('row'), may hold values from 0 to 7, as said below
Outputs:
- solution_field: float32 [3, 65536, 512], P(None, 'row', 'col')
- residual: float32 [3, 65536, 512], P(None, 'row', 'col')
The draws below stay inside these ranges and needn't reach their ends.
Inputs may be any that keep to these rules, and one draw needn't show every extreme that they name: readers[p, o] holds 4 distinct local cluster numbers of row device p; they are read by the row device whose index is p - o + 3, cyclically. `tile_slot`: slots are distinct within one cluster row; on each row device every slot is named by some tile.
All inputs are finite; a program needn't handle non-finite values.
Results may differ from the reference program's by a relative error of at most 0.0023.
Values may be sent and summed in bfloat16 or wider, within the bound.
A program may use at most 128 MiB of HBM per device.

```python
import jax
import jax.numpy as jnp
from jax import lax

TILE = 128
FIELDS = 3
CL_DEV = 8
ORB_DEV = 128
NNZ = 24
NNZ_S = 8
HALF = 3
CAP = 4
ITERS = 2
SPAN = 7
SLOTS = 28
CLUSTERS = 512
NB = 65536
ORB = 512
N_ROW = 64
N_COL = 4


def cluster_levels(key):
    return jax.random.randint(key, (CLUSTERS,), 0, 2).astype(jnp.float32)


def make_onsite(key, level, base, jitter_top):
    per_row = jnp.repeat(level, TILE)
    jitter = jax.random.uniform(key, (NB,), jnp.float32, 0.0, jitter_top)
    return 8.0 + base * per_row + jitter


def draw_onsite(key, part):
    level = cluster_levels(key)
    key = jax.random.fold_in(key, 13)
    values = make_onsite(key, level, 6.0, 2.0)
    return values.astype(jnp.float32)


def make_right_side(key, level, spread, shift, base):
    key_rank, key_noise, key_sign = jax.random.split(key, 3)
    rank = jax.random.permutation(key_rank, N_COL).astype(jnp.float32)
    tilt = 2.0 * rank / max(N_COL - 1, 1) - 1.0
    level_sign = 2.0 * level - 1.0
    noise = jax.random.uniform(key_noise, (CLUSTERS, N_COL), jnp.float32, -spread, spread)
    amplitude = 3.0 * jnp.exp(level_sign[:, None] * tilt[None, :] + noise)
    amplitude = jnp.repeat(jnp.repeat(amplitude, TILE, axis=0), ORB_DEV, axis=1)
    signs = jnp.where(jax.random.randint(key_sign, (FIELDS,), 0, 2) == 1, 1.0, -1.0).astype(jnp.float32)
    values = amplitude[None, :, :] * (base + shift * signs[:, None, None])
    return jnp.clip(values, -48.0, 48.0)


def draw_right_side(key, part):
    level = cluster_levels(key)
    key = jax.random.fold_in(key, 14)
    key_base, key_rest = jax.random.split(key)
    base = jax.random.normal(key_base, (FIELDS, NB, ORB), jnp.float32)
    values = make_right_side(key_rest, level, 0.7, 0.4, base)
    return values.astype(jnp.float32)


def draw_ks_tiles(key, part):
    key = jax.random.fold_in(key, 15)
    deviation = (NNZ * TILE) ** (-0.5)
    shape = (CLUSTERS, NNZ, TILE, TILE)
    base = jnp.clip(jax.random.normal(key, shape, jnp.float32), -5.0, 5.0)
    values = deviation * (base + 0.55)
    return values.astype(jnp.bfloat16)


def draw_readers(key, part):
    key = jax.random.fold_in(key, 11)
    scores = jax.random.randint(key, (N_ROW * SPAN, CL_DEV), 0, 1 << 20) * CL_DEV
    scores = scores + jnp.arange(CL_DEV, dtype=jnp.int32)[None, :]
    order = jnp.argsort(scores, axis=1)
    return order[:, :CAP].astype(jnp.int32).reshape(N_ROW, SPAN, CAP)


def draw_tile_slot(key, part):
    key = jax.random.fold_in(key, 12)
    scores = jax.random.randint(key, (N_ROW, SLOTS), 0, 1 << 20) * SLOTS
    scores = scores + jnp.arange(SLOTS, dtype=jnp.int32)[None, :]
    order = jnp.argsort(scores, axis=1).astype(jnp.int32)
    place = (jnp.arange(CL_DEV, dtype=jnp.int32)[:, None] * NNZ + jnp.arange(NNZ, dtype=jnp.int32)[None, :]) % SLOTS
    picked = order[:, place]
    return picked.reshape(CLUSTERS, NNZ).astype(jnp.int32)


def level_of(own_key, shape, cuts, smallest, largest):
    loudness, own = 1.0, jax.random.fold_in(own_key, 6)
    for dim, blocks in cuts:
        heights = jnp.exp(jax.random.uniform(jax.random.fold_in(own, dim), (blocks,), jnp.float32, smallest / len(cuts), largest / len(cuts)))
        loudness = loudness * jnp.repeat(heights, shape[dim] // blocks).reshape([-1 if axis == dim else 1 for axis in range(len(shape))])
    return loudness


def bell_draw(stream_key, shape, scale, reach, cuts=(), kind=jnp.bfloat16):
    gain = level_of(stream_key, shape, cuts, -0.22, 0.18) if cuts else 1.0
    result = jax.random.normal(stream_key, shape, jnp.float32) * scale * gain
    return jnp.minimum(jnp.maximum(result, -reach), reach).astype(kind)


def setup_inputs(seed: int = 0) -> dict:
    splits = jax.random.split(jax.random.key(seed), 8)
    right_side = draw_right_side(jax.random.fold_in(splits[7], 71), 0)
    onsite = draw_onsite(jax.random.fold_in(splits[7], 71), 0)
    energies = jnp.clip(-1.0 + 0.75 * jax.random.uniform(splits[2], (ORB,), jnp.float32) ** level_of(splits[2], (ORB,), ((0, 4),), -0.2, 0.2), -1.0, -0.25)
    ks_tiles = draw_ks_tiles(jax.random.fold_in(splits[7], 71), 0)
    correlation_tiles = bell_draw(splits[4], (CLUSTERS, NNZ_S, TILE, TILE), (NNZ_S * TILE) ** -0.5, 0.1875, ((0, 64),))
    tile_slot = draw_tile_slot(jax.random.fold_in(splits[7], 71), 0)
    readers = draw_readers(jax.random.fold_in(splits[7], 71), 0)
    return {"right_side": right_side, "onsite": onsite, "energies": energies, "ks_tiles": ks_tiles, "correlation_tiles": correlation_tiles, "tile_slot": tile_slot, "readers": readers}


def reference(right_side, onsite, energies, ks_tiles, correlation_tiles, tile_slot, readers):
    owner = (jnp.arange(CLUSTERS, dtype=jnp.int32) // CL_DEV)[:, None]
    offset = (tile_slot // CAP).astype(jnp.int32)
    entry = (tile_slot % CAP).astype(jnp.int32)
    source = ((owner + offset - HALF) % N_ROW).astype(jnp.int32)
    columns = (source * CL_DEV + readers[source, offset, entry]).astype(jnp.int32)

    def operate(field):
        blocks = field.astype(jnp.bfloat16).reshape(FIELDS, CLUSTERS, TILE, ORB)

        def one_cluster(index):
            picked = blocks[:, columns[index]].astype(jnp.float32)
            ks_term = jnp.einsum("kab,fkbj->faj", ks_tiles[index].astype(jnp.float32), picked)
            ov_term = jnp.einsum("kab,fkbj->faj", correlation_tiles[index].astype(jnp.float32), picked[:, :NNZ_S])
            return ks_term - ov_term * energies[None, None, :]

        coupled = lax.map(one_cluster, jnp.arange(CLUSTERS, dtype=jnp.int32))
        coupled = jnp.transpose(coupled, (1, 0, 2, 3)).reshape(FIELDS, NB, ORB)
        return onsite[None, :, None] * field + coupled

    solution_field = jnp.zeros_like(right_side)
    residual = right_side
    direction = right_side
    norm_now = jnp.sum(residual * residual, axis=(1, 2))
    for step in range(ITERS):
        image = operate(direction)
        alpha = (norm_now / jnp.sum(direction * image, axis=(1, 2)))[:, None, None]
        solution_field = solution_field + alpha * direction
        residual = residual - alpha * image
        norm_next = jnp.sum(residual * residual, axis=(1, 2))
        direction = residual + (norm_next / norm_now)[:, None, None] * direction
        norm_now = norm_next
    return solution_field, residual
```

```python
import functools

import jax
import jax.numpy as jnp
from jax import lax
from jax.experimental import pallas as pl
from jax.experimental.pallas import tpu as pltpu
from jax.sharding import PartitionSpec as P

MESH = pl.DeviceIdType.MESH
F32 = jnp.float32
BF16 = jnp.bfloat16
ITERS = 2
SIZES = {"x": 4, "y": 4, "z": 8, "core": 2}
GROUPS = (("x", "y"), ("z", "core"))
STEP = 1.0 / 12.0
OTHERS = (0, 6, 1, 5, 2, 4)


def members(axes, here):
    count, mine = 1, 0
    for a in axes:
        count *= SIZES[a]
        mine = mine * SIZES[a] + here[a]
    found = []
    for distance in range(1, count):
        there, rest = dict(here), lax.rem(mine + distance, count)
        for a in reversed(axes):
            there[a] = lax.rem(rest, SIZES[a])
            rest = rest // SIZES[a]
        found.append(((there["y"] * SIZES["z"] + there["z"]) * SIZES["core"] + there["core"], there["x"]))
    return found


def kernel(
    right_hbm, onsite_ref, energies_ref, ks_hbm, corr_hbm, slot_ref, readers_ref,
    x_hbm, res_hbm,
    r0a, r0b, r0c, y, dd, im, ob, wb, kc, ks, corr, gath, pack, inv_v, inv_s, sums,
    part1, got1a, part1b, got1b, part2, got2a, part2b, got2b,
    load_sem, inv_sem, out_sem, send_sem, recv_sem, psend, precv,
):
    r0 = (r0a, r0b, r0c)
    fields = len(r0)
    clusters = 8
    width = 128
    slots = 28
    n_row = lax.axis_size("row")
    row, col = lax.axis_index("row"), lax.axis_index("col")
    here = {"x": col, "y": row // 16, "z": lax.rem(row // 2, 8), "core": lax.rem(row, 2)}
    groups = [members(g, here) for g in GROUPS]
    targets = {o: (lax.rem(row + 3 - o + n_row, n_row), col) for o in OTHERS}

    barrier = pltpu.get_barrier_semaphore()
    everyone = list(targets.values()) + groups[0] + groups[1]
    for device in everyone:
        pl.semaphore_signal(barrier, 1, device_id=device, device_id_type=MESH)

    loads = [pltpu.make_async_copy(right_hbm.at[f], r0[f], load_sem.at[f]) for f in range(fields)]
    loads.append(pltpu.make_async_copy(ks_hbm, ks.at[pl.ds(0, 192)], load_sem.at[3]))
    loads.append(pltpu.make_async_copy(corr_hbm, corr.at[pl.ds(0, 64)], load_sem.at[4]))
    for load in loads:
        load.start()

    lane = lax.broadcasted_iota(jnp.int32, (8, 128), 1)
    first = lax.broadcasted_iota(jnp.int32, (8, 128), 0)
    at_ks = jnp.full((8, 128), 192, jnp.int32)
    at_corr = jnp.full((8, 128), 64, jnp.int32)
    for k in range(24):
        hit = lane == slot_ref[:, k : k + 1]
        at_ks = jnp.where(hit, first * 24 + k, at_ks)
        if k < 8:
            at_corr = jnp.where(hit, first * 8 + k, at_corr)
    inv_v[0:8] = at_ks
    inv_v[8:16] = at_corr
    inv_copy = pltpu.make_async_copy(inv_v, inv_s, inv_sem)
    inv_copy.start()
    ks[192] = jnp.zeros((width, width), BF16)
    corr[64] = jnp.zeros((width, width), BF16)
    for c in range(clusters):
        ob[c] = jnp.transpose(
            jnp.broadcast_to(onsite_ref[c : c + 1, :], (width, width))
        )
    sums[...] = jnp.zeros_like(sums)

    def copies(phase):
        return {
            o: pltpu.make_async_remote_copy(
                src_ref=pack.at[phase, o],
                dst_ref=gath.at[phase, pl.ds(4 * o, 4)],
                send_sem=send_sem.at[phase, o],
                recv_sem=recv_sem.at[phase, o],
                device_id=targets[o],
                device_id_type=MESH,
            )
            for o in OTHERS
        }

    sends = [copies(phase) for phase in range(2 * fields)]

    def fill(phase, o, read):
        def one(s, _):
            block = read(readers_ref[0, o, s])
            if o == 3:
                gath[phase, 12 + s] = block
            else:
                pack[phase, o, s] = block
            return 0

        lax.fori_loop(0, 4, one, 0)

    def from_right(f):
        return lambda c: r0[f][c].astype(BF16)

    def from_w(f):
        return lambda c: wb[f, c]

    def send(phase):
        for o in OTHERS:
            sends[phase][o].start()

    for f in range(fields):
        loads[f].wait()
        for o in OTHERS:
            fill(f, o, from_right(f))
        if f == 0:
            pl.semaphore_wait(barrier, len(everyone))
        send(f)
    for f in range(fields):
        fill(f, 3, from_right(f))

    loads[3].wait()
    loads[4].wait()
    inv_copy.wait()

    def lay(c, _):
        for s in range(slots):
            kc[pl.ds(c * 256, width), s * width : (s + 1) * width] = ks[inv_s[c, s]]
            kc[pl.ds(c * 256 + width, width), s * width : (s + 1) * width] = corr[inv_s[8 + c, s]]
        return 0

    lax.fori_loop(0, clusters, lay, 0)
    energies = energies_ref[0:1, :]

    def fold(block):
        return jnp.sum(block.reshape(width // 8, 8, width), axis=0)

    def product(phase, then):
        block = gath[phase].reshape(slots * width, width)

        def part(i, _):
            out = jnp.dot(kc[pl.ds(pl.multiple_of(i * 1024, 1024), 1024), :], block, preferred_element_type=F32)
            for j in range(4):
                then(4 * i + j, out[j * 256 : j * 256 + 128] - energies * out[j * 256 + 128 : j * 256 + 256])
            return 0

        lax.fori_loop(0, 2, part, 0)

    def reduce_start(mine, got, which, stage):
        found = []
        group = groups[stage]
        for distance, device in enumerate(group, 1):
            copy = pltpu.make_async_remote_copy(
                src_ref=mine,
                dst_ref=got.at[len(group) - distance],
                send_sem=psend.at[which, stage, distance],
                recv_sem=precv.at[which, stage, len(group) - distance],
                device_id=device,
                device_id_type=MESH,
            )
            copy.start()
            found.append(copy)
        return found

    for f in range(fields):
        for o in OTHERS:
            sends[f][o].wait_recv()

        def first_then(c, coupled):
            r = r0[f][c]
            image = ob[c] * r + coupled
            y[f, c] = image
            wb[f, c] = (r - STEP * image).astype(BF16)
            sums[f] += fold(r * r)
            sums[3 + f] += fold(r * image)
            sums[6 + f] += fold(image * image)

        product(f, first_then)
        for o in OTHERS + (3,):
            fill(fields + f, o, from_w(f))
        if f < fields - 1:
            send(fields + f)
    for i in range(9):
        part1[i : i + 1, :] = jnp.sum(sums[i], axis=0, keepdims=True)
    part1[9:16, :] = jnp.zeros((7, 128), F32)
    stage_a = reduce_start(part1, got1a, 0, 0)
    for copy in stage_a:
        copy.wait_recv()
    part1b[...] = part1[...] + jnp.sum(got1a[...], axis=0)
    stage_b = reduce_start(part1b, got1b, 0, 1)
    send(2 * fields - 1)

    def second_then_of(f):
        def second_then(c, coupled):
            im[f, c] = ob[c] * (r0[f][c] - STEP * y[f, c]) + coupled

        return second_then

    for o in OTHERS:
        sends[fields][o].wait_recv()
    product(fields, second_then_of(0))

    for copy in stage_b:
        copy.wait_recv()
    whole = jnp.sum(part1b[...] + jnp.sum(got1b[...], axis=0), axis=1, keepdims=True)
    alpha, beta, gain, rr1 = [], [], [], []
    for f in range(fields):
        rr0, b0, yy = whole[f : f + 1], whole[3 + f : 4 + f], whole[6 + f : 7 + f]
        a = rr0 / b0
        n = rr0 + a * (a * yy - 2.0 * b0)
        alpha.append(a)
        rr1.append(n)
        beta.append(n / rr0)
        gain.append(a / STEP)

    for f in range(fields):
        if f > 0:
            for o in OTHERS:
                sends[fields + f][o].wait_recv()
            product(fields + f, second_then_of(f))
        keep = 1.0 - gain[f] + beta[f]

        def combine(c, total):
            r, image = r0[f][c], y[f, c]
            later = r - alpha[f] * image
            direction = later + beta[f] * r
            image = gain[f] * im[f, c] + keep * image
            y[f, c] = later
            dd[f, c] = direction
            im[f, c] = image
            return total + fold(direction * image)

        total = lax.fori_loop(0, clusters, combine, jnp.zeros((8, 128), F32))
        part2[f : f + 1, :] = jnp.sum(total, axis=0, keepdims=True)
    part2[3:8, :] = jnp.zeros((5, 128), F32)

    last_a = reduce_start(part2, got2a, 1, 0)
    for copy in last_a:
        copy.wait_recv()
    part2b[...] = part2[...] + jnp.sum(got2a[...], axis=0)
    last_b = reduce_start(part2b, got2b, 1, 1)
    for copy in last_b:
        copy.wait_recv()
    whole = jnp.sum(part2b[...] + jnp.sum(got2b[...], axis=0), axis=1, keepdims=True)

    outs = []
    for f in range(fields):
        step = rr1[f] / whole[f : f + 1]

        def finish(c, _):
            dd[f, c] = alpha[f] * r0[f][c] + step * dd[f, c]
            y[f, c] = y[f, c] - step * im[f, c]
            return 0

        lax.fori_loop(0, clusters, finish, 0)
        outs.append(pltpu.make_async_copy(dd.at[f], x_hbm.at[f], out_sem.at[f]))
        outs.append(pltpu.make_async_copy(y.at[f], res_hbm.at[f], out_sem.at[3 + f]))
        outs[-2].start()
        outs[-1].start()
    for phase in sends:
        for copy in phase.values():
            copy.wait_send()
    for copy in stage_a + stage_b + last_a + last_b:
        copy.wait_send()
    for copy in outs:
        copy.wait()


def body(right_side, onsite, energies, ks_tiles, correlation_tiles, tile_slot, readers):
    fields = right_side.shape[0]
    any_, vmem, smem = pl.ANY, pltpu.VMEM, pltpu.SMEM
    spaces = (any_, vmem, vmem, any_, any_, vmem, smem)
    field = (fields, 8, 128, 128)
    scratch = [
        pltpu.VMEM(field[1:], F32),
        pltpu.VMEM(field[1:], F32),
        pltpu.VMEM(field[1:], F32),
        pltpu.VMEM(field, F32),
        pltpu.VMEM(field, F32),
        pltpu.VMEM(field, F32),
        pltpu.VMEM(field[1:], F32),
        pltpu.VMEM(field, BF16),
        pltpu.VMEM((2048, 3584), BF16),
        pltpu.VMEM((193, 128, 128), BF16),
        pltpu.VMEM((65, 128, 128), BF16),
        pltpu.VMEM((6, 28, 128, 128), BF16),
        pltpu.VMEM((6, 7, 4, 128, 128), BF16),
        pltpu.VMEM((16, 128), jnp.int32),
        pltpu.SMEM((16, 128), jnp.int32),
        pltpu.VMEM((9, 8, 128), F32),
        pltpu.VMEM((16, 128), F32),
        pltpu.VMEM((15, 16, 128), F32),
        pltpu.VMEM((16, 128), F32),
        pltpu.VMEM((15, 16, 128), F32),
        pltpu.VMEM((8, 128), F32),
        pltpu.VMEM((15, 8, 128), F32),
        pltpu.VMEM((8, 128), F32),
        pltpu.VMEM((15, 8, 128), F32),
        pltpu.SemaphoreType.DMA((5,)),
        pltpu.SemaphoreType.DMA,
        pltpu.SemaphoreType.DMA((6,)),
        pltpu.SemaphoreType.DMA((6, 7)),
        pltpu.SemaphoreType.DMA((6, 7)),
        pltpu.SemaphoreType.DMA((2, 2, 16)),
        pltpu.SemaphoreType.DMA((2, 2, 16)),
    ]
    x, res = pl.pallas_call(
        kernel,
        out_shape=(jax.ShapeDtypeStruct(field, F32),) * 2,
        in_specs=[pl.BlockSpec(memory_space=s) for s in spaces],
        out_specs=(pl.BlockSpec(memory_space=any_),) * 2,
        scratch_shapes=scratch,
        compiler_params=pltpu.CompilerParams(
            collective_id=0, has_side_effects=True, vmem_limit_bytes=56 << 20
        ),
    )(
        right_side.reshape(field),
        onsite.reshape(8, 128),
        energies.reshape(1, 128),
        ks_tiles.reshape(192, 128, 128),
        correlation_tiles.reshape(64, 128, 128),
        tile_slot,
        readers,
    )
    return x.reshape(right_side.shape), res.reshape(right_side.shape)


def solution(mesh):
    placed = (
        P(None, "row", "col"),
        P("row"),
        P("col"),
        P("row", None, None, None),
        P("row", None, None, None),
        P("row", None),
        P("row", None, None),
    )
    return jax.shard_map(
        body,
        mesh=mesh,
        in_specs=placed,
        out_specs=(P(None, "row", "col"), P(None, "row", "col")),
        check_vma=False,
    )
```

```python
import jax
import jax.numpy as jnp
from jax import lax
from jax.experimental import pallas as pl
from jax.experimental.pallas import tpu as pltpu
from jax.sharding import PartitionSpec as P

MESH = pl.DeviceIdType.MESH
F32 = jnp.float32
BF16 = jnp.bfloat16
SIZES = {"x": 4, "y": 4, "z": 8, "core": 2}
GROUPS = (("x", "y"), ("z", "core"))
STEP = 1.0 / 12.0
OWN, SIB, OUT2, IN2, IN3, OUT1, OUT3 = range(7)
FULL = 7


def members(axes, here):
    count, mine = 1, 0
    for a in axes:
        count *= SIZES[a]
        mine = mine * SIZES[a] + here[a]
    found = []
    for distance in range(1, count):
        there, rest = dict(here), lax.rem(mine + distance, count)
        for a in reversed(axes):
            there[a] = lax.rem(rest, SIZES[a])
            rest = rest // SIZES[a]
        found.append(((there["y"] * SIZES["z"] + there["z"]) * SIZES["core"] + there["core"], there["x"]))
    return found


def kernel(
    right_hbm, onsite_ref, energies_ref, ks_hbm, corr_hbm, slot_ref, readers_ref,
    y, z, coef_ref,
    r0a, r0b, r0c, ob, vb, kc, ks, corr, acc, gath, pack,
    full0, full1, full2, full3, full4,
    inv_v, inv_s, mine_v, mine_s, theirs_v, theirs_s, sums,
    part, got, partb, gotb,
    load_sem, table_sem, send_sem, recv_sem, psend, precv,
):
    r0 = (r0a, r0b, r0c)
    full = (full0, full1, full2, full3, full4)
    fields = len(r0)
    last = 2 * fields - 1
    clusters, width, slots = 8, 128, 28
    n_row = lax.axis_size("row")
    row, col = lax.axis_index("row"), lax.axis_index("col")
    core = lax.rem(row, 2)
    s = 2 * core - 1
    here = {"x": col, "y": row // 16, "z": lax.rem(row // 2, 8), "core": core}
    groups = [members(g, here) for g in GROUPS]

    def away(d):
        return (lax.rem(row + d + n_row, n_row), col)

    barrier = pltpu.get_barrier_semaphore()
    everyone = [away(d * s) for d in (-3, -2, -1, 1, 2, 3)] + groups[0] + groups[1]
    for device in everyone:
        pl.semaphore_signal(barrier, 1, device_id=device, device_id_type=MESH)

    loads = [pltpu.make_async_copy(right_hbm.at[f], r0[f], load_sem.at[f]) for f in range(fields)]
    loads.append(pltpu.make_async_copy(ks_hbm, ks.at[pl.ds(0, 192)], load_sem.at[3]))
    loads.append(pltpu.make_async_copy(corr_hbm, corr.at[pl.ds(0, 64)], load_sem.at[4]))
    for load in loads:
        load.start()

    mine_v[...] = jnp.zeros_like(mine_v)
    mine_v[0:4, 0:7] = readers_ref[...]
    mine_copy = pltpu.make_async_copy(mine_v, mine_s, table_sem.at[0])
    mine_copy.start()

    lane = lax.broadcasted_iota(jnp.int32, (8, 128), 1)
    first = lax.broadcasted_iota(jnp.int32, (8, 128), 0)
    at_ks = jnp.full((8, 128), 192, jnp.int32)
    at_corr = jnp.full((8, 128), 64, jnp.int32)
    for k in range(24):
        hit = lane == slot_ref[:, k : k + 1]
        at_ks = jnp.where(hit, first * 24 + k, at_ks)
        if k < 8:
            at_corr = jnp.where(hit, first * 8 + k, at_corr)
    inv_v[0:8] = at_ks
    inv_v[8:16] = at_corr
    inv_copy = pltpu.make_async_copy(inv_v, inv_s, table_sem.at[1])
    inv_copy.start()
    ks[192] = jnp.zeros((width, width), BF16)
    corr[64] = jnp.zeros((width, width), BF16)
    sums[...] = jnp.zeros_like(sums)

    def remote(phase, kind, src, dst, d):
        return pltpu.make_async_remote_copy(
            src_ref=src,
            dst_ref=dst,
            send_sem=send_sem.at[phase, kind],
            recv_sem=recv_sem.at[phase, kind],
            device_id=away(d * s),
            device_id_type=MESH,
        )

    straight = {SIB: -1, IN2: -2, IN3: -3, OUT1: 1, OUT2: 2, OUT3: 3}
    copies = []
    for phase in range(2 * fields):
        passed = phase < last
        found = {}
        for kind, d in straight.items():
            if passed and kind == OUT2:
                continue
            hop = d - 2 if passed and kind in (OUT1, OUT3) else d
            found[kind] = remote(phase, kind, pack.at[phase, kind], gath.at[phase, pl.ds(4 * kind, 4)], hop)
        if passed:
            found[FULL] = remote(phase, FULL, vb.at[phase], full[phase], 2)
        copies.append(found)
    table = pltpu.make_async_remote_copy(
        src_ref=mine_v,
        dst_ref=theirs_v,
        send_sem=table_sem.at[2],
        recv_sem=table_sem.at[3],
        device_id=away(2 * s),
        device_id_type=MESH,
    )

    def fill(phase, kind, read, names, o):
        def one(i, _):
            block = read(names[i, o])
            if kind in (OWN, FULL):
                gath[phase, (4 * OWN if kind == OWN else 4 * OUT2) + i] = block
            else:
                pack[phase, kind, i] = block
            return 0

        lax.fori_loop(0, 4, one, 0)

    def fill_mine(phase, kinds):
        for kind in kinds:
            o = 3 if kind == OWN else 3 - straight[kind] * s
            fill(phase, kind, lambda c: vb[phase, c], mine_s, o)

    def start(phase, kinds):
        for kind in kinds:
            copies[phase][kind].start()

    def wait(phase, kinds):
        for kind in kinds:
            copies[phase][kind].wait_recv()

    def send_out(phase):
        start(phase, (FULL,))
        fill_mine(phase, (SIB, IN3, IN2))
        start(phase, (IN3, IN2, SIB))

    def pass_on(phase):
        wait(phase, (FULL,))
        read = lambda c: full[phase][c]
        fill(phase, OUT3, read, theirs_s, 3 - 3 * s)
        start(phase, (OUT3,))
        fill(phase, OUT1, read, theirs_s, 3 - s)
        start(phase, (OUT1,))
        fill(phase, FULL, read, theirs_s, 3 - 2 * s)

    def halve(f):
        def one(c, _):
            vb[f, c] = r0[f][c].astype(BF16)
            return 0

        lax.fori_loop(0, clusters, one, 0)

    loads[0].wait()
    halve(0)
    mine_copy.wait()
    fill_mine(0, (SIB, IN3, IN2))
    pl.semaphore_wait(barrier, len(everyone))
    table.start()
    start(0, (FULL, IN3, IN2, SIB))
    loads[1].wait()
    halve(1)
    send_out(1)
    loads[2].wait()
    halve(2)
    fill_mine(2, (SIB, IN3, IN2))
    for f in range(fields):
        fill_mine(f, (OWN,))
    for c in range(clusters):
        ob[c] = jnp.transpose(jnp.broadcast_to(onsite_ref[c : c + 1, :], (width, width)))

    loads[3].wait()
    loads[4].wait()
    inv_copy.wait()
    offsets = [3, 3 - s, 3 - 2 * s, 3 + 2 * s, 3 - 3 * s, 3 + s, 3 + 3 * s]

    def lay(c, _):
        for kind in range(7):
            for i in range(4):
                slot = 4 * offsets[kind] + i
                at = slice((4 * kind + i) * width, (4 * kind + i + 1) * width)
                kc[pl.ds(c * 256, width), at] = ks[inv_s[c, slot]]
                kc[pl.ds(c * 256 + width, width), at] = corr[inv_s[8 + c, slot]]
        return 0

    lax.fori_loop(0, clusters, lay, 0)
    table.wait_recv()
    theirs_copy = pltpu.make_async_copy(theirs_v, theirs_s, table_sem.at[4])
    theirs_copy.start()
    theirs_copy.wait()
    energies = energies_ref[0:1, :]

    def fold(block):
        return jnp.sum(block.reshape(width // 8, 8, width), axis=0)

    def product(phase, a, b, where, fresh, then=None):
        block = gath[phase, 4 * a : 4 * b].reshape(4 * (b - a) * width, width)

        def part(i, _):
            at = pl.ds(pl.multiple_of(i * 1024, 1024), 1024)
            out = jnp.dot(kc[at, 4 * a * width : 4 * b * width], block, preferred_element_type=F32)
            if not fresh:
                out = out + acc[where, at, :]
            if then is None:
                acc[where, at, :] = out
            else:
                for j in range(4):
                    then(4 * i + j, out[j * 256 : j * 256 + 128] - energies * out[j * 256 + 128 : j * 256 + 256])
            return 0

        lax.fori_loop(0, 2, part, 0)

    def reduce_start(mine, got, stage):
        group = groups[stage]
        for distance, device in enumerate(group, 1):
            pltpu.make_async_remote_copy(
                src_ref=mine,
                dst_ref=got.at[len(group) - distance],
                send_sem=psend.at[stage],
                recv_sem=precv.at[stage],
                device_id=device,
                device_id_type=MESH,
            ).start()
        return pltpu.make_async_remote_copy(
            src_ref=got,
            dst_ref=got,
            send_sem=psend.at[stage],
            recv_sem=precv.at[stage],
            device_id=group[0],
            device_id_type=MESH,
        )

    def first_then_of(f):
        def first_then(c, coupled):
            r = r0[f][c]
            image = ob[c] * r + coupled
            y[f, c] = image
            vb[fields + f, c] = (r - STEP * image).astype(BF16)
            sums[f] += fold(r * r)
            sums[3 + f] += fold(r * image)
            sums[6 + f] += fold(image * image)

        return first_then

    def second_then_of(f):
        def second_then(c, coupled):
            r = r0[f][c]
            w = r - STEP * y[f, c]
            image = ob[c] * w + coupled
            z[f, c] = image
            sums[9 + f] += fold(w * image)
            sums[12 + f] += fold(r * image)

        return second_then

    def early(phase, where):
        wait(phase, (SIB, IN2, IN3))
        product(phase, OWN, OUT1, where, True)

    def late(phase, where, then):
        wait(phase, (OUT1, OUT3))
        product(phase, OUT1, 7, where, False, then)

    pass_on(0)
    start(2, (FULL, IN3, IN2, SIB))
    early(0, 0)
    pass_on(1)
    late(0, 0, first_then_of(0))
    send_out(3)
    early(1, 1)
    pass_on(2)
    late(1, 1, first_then_of(1))
    send_out(4)
    fill_mine(3, (OWN,))
    early(2, 2)
    pass_on(3)
    late(2, 2, first_then_of(2))
    fill_mine(last, (OUT3, OUT2))
    start(last, (OUT3, OUT2))

    fill_mine(last, (SIB, OUT1, IN2, IN3, OWN))
    start(last, (SIB,))
    early(3, 0)
    pass_on(4)
    start(last, (OUT1, IN2, IN3))
    fill_mine(4, (OWN,))
    early(4, 1)
    late(3, 0, second_then_of(0))
    wait(last, (SIB,))
    product(last, OWN, OUT2, 2, True)
    wait(last, (OUT2,))
    product(last, OUT2, IN2, 2, False)
    wait(last, (OUT3,))
    product(last, OUT3, 7, 2, False)
    late(4, 1, second_then_of(1))
    wait(last, (OUT1,))
    product(last, OUT1, OUT3, 2, False)
    wait(last, (IN2,))
    product(last, IN2, IN3, 2, False)
    wait(last, (IN3,))
    product(last, IN3, OUT1, 2, False, second_then_of(2))

    corner = lax.broadcasted_iota(jnp.int32, (16, 128), 0) == lax.broadcasted_iota(jnp.int32, (16, 128), 1)
    column = jnp.sum(jnp.sum(sums[...], axis=1), axis=1, keepdims=True)
    part[...] = jnp.sum(jnp.where(corner, column, 0.0), axis=0, keepdims=True)
    stage_a = reduce_start(part, got, 0)
    for phase in copies:
        for copy in phase.values():
            copy.wait_send()
    table.wait_send()
    stage_a.wait_recv()
    partb[...] = part[...] + jnp.sum(got[...], axis=0)
    stage_b = reduce_start(partb, gotb, 1)
    stage_a.wait_send()
    stage_b.wait_recv()
    row_sums = partb[...] + jnp.sum(gotb[...], axis=0)
    whole = jnp.sum(jnp.where(corner, row_sums, 0.0), axis=1, keepdims=True)
    rr0, b0, yy, wz, rz = (whole[3 * i : 3 * i + 3] for i in range(5))
    alpha = rr0 / b0
    rr1 = rr0 + alpha * (alpha * yy - 2.0 * b0)
    gain = alpha / STEP
    keep = 1.0 - gain + rr1 / rr0
    bend = gain * gain * wz + gain * keep * (b0 - STEP * yy + rz) + keep * keep * b0
    step = rr1 / bend
    given = (alpha + step * (gain + keep), -step * gain * STEP, -(alpha + step * keep), -step * gain)
    for i, value in enumerate(given):
        coef_ref[3 * i : 3 * i + 3, :] = jnp.broadcast_to(value, (3, 128))
    coef_ref[12:16, :] = jnp.zeros((4, 128), F32)
    stage_b.wait_send()


def finish(right_hbm, y, z, coef_ref, x_hbm, res_hbm, r0, x, res, load_sem, out_sem):
    fields = y.shape[0]
    loads = [pltpu.make_async_copy(right_hbm.at[f], r0.at[f], load_sem.at[f]) for f in range(fields)]
    for load in loads:
        load.start()
    outs = []
    for f in range(fields):
        a, b, c, d = (coef_ref[3 * i + f : 3 * i + f + 1, :] for i in range(4))
        loads[f].wait()
        for half in range(2):

            def one(i, _):
                i = 4 * half + i
                r, image = r0[f, i], y[f, i]
                x[f, i] = a * r + b * image
                res[f, i] = r + c * image + d * z[f, i]
                return 0

            lax.fori_loop(0, 4, one, 0)
            at = pl.ds(4 * half, 4)
            for array, out, which in ((x, x_hbm, 0), (res, res_hbm, 1)):
                outs.append(pltpu.make_async_copy(array.at[f, at], out.at[f, at], out_sem.at[which, f, half]))
                outs[-1].start()
    for out in outs:
        out.wait()


def body(right_side, onsite, energies, ks_tiles, correlation_tiles, tile_slot, readers):
    fields = right_side.shape[0]
    any_, vmem = pl.ANY, pltpu.VMEM
    spaces = (any_, vmem, vmem, any_, any_, vmem, vmem)
    field = (fields, 8, 128, 128)
    scratch = [
        pltpu.VMEM(field[1:], F32),
        pltpu.VMEM(field[1:], F32),
        pltpu.VMEM(field[1:], F32),
        pltpu.VMEM(field[1:], F32),
        pltpu.VMEM((6, 8, 128, 128), BF16),
        pltpu.VMEM((2048, 3584), BF16),
        pltpu.VMEM((193, 128, 128), BF16),
        pltpu.VMEM((65, 128, 128), BF16),
        pltpu.VMEM((3, 2048, 128), F32),
        pltpu.VMEM((6, 28, 128, 128), BF16),
        pltpu.VMEM((6, 7, 4, 128, 128), BF16),
        *[pltpu.VMEM((8, 128, 128), BF16) for _ in range(5)],
        pltpu.VMEM((16, 128), jnp.int32),
        pltpu.SMEM((16, 128), jnp.int32),
        pltpu.VMEM((8, 128), jnp.int32),
        pltpu.SMEM((8, 128), jnp.int32),
        pltpu.VMEM((8, 128), jnp.int32),
        pltpu.SMEM((8, 128), jnp.int32),
        pltpu.VMEM((16, 8, 128), F32),
        pltpu.VMEM((1, 128), F32),
        pltpu.VMEM((15, 1, 128), F32),
        pltpu.VMEM((1, 128), F32),
        pltpu.VMEM((15, 1, 128), F32),
        pltpu.SemaphoreType.DMA((5,)),
        pltpu.SemaphoreType.DMA((5,)),
        pltpu.SemaphoreType.DMA((6, 8)),
        pltpu.SemaphoreType.DMA((6, 8)),
        pltpu.SemaphoreType.DMA((2,)),
        pltpu.SemaphoreType.DMA((2,)),
    ]
    y, z, coef = pl.pallas_call(
        kernel,
        out_shape=(
            pltpu.VMEM(field, F32),
            pltpu.VMEM(field, F32),
            pltpu.VMEM((16, 128), F32),
        ),
        in_specs=[pl.BlockSpec(memory_space=s) for s in spaces],
        out_specs=(pl.BlockSpec(memory_space=vmem),) * 3,
        scratch_shapes=scratch,
        compiler_params=pltpu.CompilerParams(
            collective_id=0, has_side_effects=True, vmem_limit_bytes=59 << 20
        ),
    )(
        right_side.reshape(field),
        onsite.reshape(8, 128),
        energies.reshape(1, 128),
        ks_tiles.reshape(192, 128, 128),
        correlation_tiles.reshape(64, 128, 128),
        tile_slot,
        readers.reshape(7, 4).T,
    )
    x, res = pl.pallas_call(
        finish,
        out_shape=(jax.ShapeDtypeStruct(field, F32),) * 2,
        in_specs=[pl.BlockSpec(memory_space=s) for s in (any_, vmem, vmem, vmem)],
        out_specs=(pl.BlockSpec(memory_space=any_),) * 2,
        scratch_shapes=[pltpu.VMEM(field, F32) for _ in range(3)]
        + [pltpu.SemaphoreType.DMA((3,)), pltpu.SemaphoreType.DMA((2, 3, 2))],
        compiler_params=pltpu.CompilerParams(vmem_limit_bytes=24 << 20),
    )(right_side.reshape(field), y, z, coef)
    return x.reshape(right_side.shape), res.reshape(right_side.shape)


def solution(mesh):
    placed = (
        P(None, "row", "col"),
        P("row"),
        P("col"),
        P("row", None, None, None),
        P("row", None, None, None),
        P("row", None),
        P("row", None, None),
    )
    return jax.shard_map(
        body,
        mesh=mesh,
        in_specs=placed,
        out_specs=(P(None, "row", "col"), P(None, "row", "col")),
        check_vma=False,
    )
```

```python
import jax
import jax.numpy as jnp
from jax import lax
from jax.experimental import pallas as pl
from jax.experimental.pallas import tpu as pltpu
from jax.sharding import PartitionSpec as P

MESH = pl.DeviceIdType.MESH
F32 = jnp.float32
BF16 = jnp.bfloat16
SIZES = {"x": 4, "y": 4, "z": 8, "core": 2}
GROUPS = (("x", "y"), ("z", "core"))
STEP = 1.0 / 12.0
OWN, SIB, OUT2, IN2, IN3, OUT1, OUT3 = range(7)
FULL = 7


def members(axes, here):
    count, mine = 1, 0
    for a in axes:
        count *= SIZES[a]
        mine = mine * SIZES[a] + here[a]
    found = []
    for distance in range(1, count):
        there, rest = dict(here), lax.rem(mine + distance, count)
        for a in reversed(axes):
            there[a] = lax.rem(rest, SIZES[a])
            rest = rest // SIZES[a]
        found.append(((there["y"] * SIZES["z"] + there["z"]) * SIZES["core"] + there["core"], there["x"]))
    return found


def kernel(
    right_hbm, onsite_ref, energies_ref, ks_hbm, corr_hbm, slot_ref, readers_ref,
    r0a, r0b, r0c, y, z, coef_ref,
    ob, vb, kc, ks, corr, acc, gath, pack,
    full0, full1, full2, full3, full4, full5,
    inv_v, inv_s, mine_v, mine_s, theirs_v, theirs_s, sums,
    part, got, partb, gotb,
    load_sem, table_sem, send_sem, recv_sem, psend, precv,
):
    r0 = (r0a, r0b, r0c)
    full = (full0, full1, full2, full3, full4, full5)
    fields = len(r0)
    last = 2 * fields - 1
    clusters, width, slots = 8, 128, 28
    n_row = lax.axis_size("row")
    row, col = lax.axis_index("row"), lax.axis_index("col")
    core = lax.rem(row, 2)
    s = 2 * core - 1
    here = {"x": col, "y": row // 16, "z": lax.rem(row // 2, 8), "core": core}
    groups = [members(g, here) for g in GROUPS]

    def away(d):
        return (lax.rem(row + d + n_row, n_row), col)

    barrier = pltpu.get_barrier_semaphore()
    everyone = [away(d * s) for d in (-3, -2, -1, 1, 2)] + groups[0] + groups[1]
    for device in everyone:
        pl.semaphore_signal(barrier, 1, device_id=device, device_id_type=MESH)

    loads = [pltpu.make_async_copy(right_hbm.at[f], r0[f], load_sem.at[f]) for f in range(fields)]
    loads.append(pltpu.make_async_copy(ks_hbm, ks.at[pl.ds(0, 192)], load_sem.at[3]))
    loads.append(pltpu.make_async_copy(corr_hbm, corr.at[pl.ds(0, 64)], load_sem.at[4]))
    for load in loads:
        load.start()

    mine_v[...] = jnp.zeros_like(mine_v)
    mine_v[0:4, 0:7] = readers_ref[...]
    mine_copy = pltpu.make_async_copy(mine_v, mine_s, table_sem.at[0])
    mine_copy.start()

    lane = lax.broadcasted_iota(jnp.int32, (8, 128), 1)
    first = lax.broadcasted_iota(jnp.int32, (8, 128), 0)
    at_ks = jnp.full((8, 128), 192, jnp.int32)
    at_corr = jnp.full((8, 128), 64, jnp.int32)
    for k in range(24):
        hit = lane == slot_ref[:, k : k + 1]
        at_ks = jnp.where(hit, first * 24 + k, at_ks)
        if k < 8:
            at_corr = jnp.where(hit, first * 8 + k, at_corr)
    inv_v[0:8] = at_ks
    inv_v[8:16] = at_corr
    inv_copy = pltpu.make_async_copy(inv_v, inv_s, table_sem.at[1])
    inv_copy.start()
    ks[192] = jnp.zeros((width, width), BF16)
    corr[64] = jnp.zeros((width, width), BF16)
    sums[...] = jnp.zeros_like(sums)

    def remote(phase, kind, src, dst, d):
        return pltpu.make_async_remote_copy(
            src_ref=src,
            dst_ref=dst,
            send_sem=send_sem.at[phase, kind],
            recv_sem=recv_sem.at[phase, kind],
            device_id=away(d * s),
            device_id_type=MESH,
        )

    straight = {SIB: -1, IN2: -2, IN3: -3, OUT1: 1, OUT2: 2, OUT3: 3}
    hops = {SIB: -1, IN2: -2, IN3: -3, OUT1: -1, OUT3: 1}
    copies = []
    for phase in range(2 * fields):
        found = {
            kind: remote(phase, kind, pack.at[phase, kind], gath.at[phase, pl.ds(4 * kind, 4)], d)
            for kind, d in hops.items()
        }
        found[FULL] = remote(phase, FULL, vb.at[phase], full[phase], 2)
        copies.append(found)
    table = pltpu.make_async_remote_copy(
        src_ref=mine_v,
        dst_ref=theirs_v,
        send_sem=table_sem.at[2],
        recv_sem=table_sem.at[3],
        device_id=away(2 * s),
        device_id_type=MESH,
    )

    def fill(phase, kind, read, names, o):
        def one(i, _):
            block = read(names[i, o])
            if kind in (OWN, FULL):
                gath[phase, (4 * OWN if kind == OWN else 4 * OUT2) + i] = block
            else:
                pack[phase, kind, i] = block
            return 0

        lax.fori_loop(0, 4, one, 0)

    def fill_mine(phase, kinds):
        for kind in kinds:
            o = 3 if kind == OWN else 3 - straight[kind] * s
            fill(phase, kind, lambda c: vb[phase, c], mine_s, o)

    def start(phase, kinds):
        for kind in kinds:
            copies[phase][kind].start()

    def wait(phase, kinds):
        for kind in kinds:
            copies[phase][kind].wait_recv()

    INWARD = (IN3, IN2, SIB)

    def pass_on(phase):
        wait(phase, (FULL,))
        read = lambda c: full[phase][c]
        fill(phase, OUT3, read, theirs_s, 3 - 3 * s)
        start(phase, (OUT3,))
        fill(phase, OUT1, read, theirs_s, 3 - s)
        start(phase, (OUT1,))
        fill(phase, FULL, read, theirs_s, 3 - 2 * s)

    def halve(f):
        def one(c, _):
            vb[f, c] = r0[f][c].astype(BF16)
            return 0

        lax.fori_loop(0, clusters, one, 0)

    loads[0].wait()
    halve(0)
    mine_copy.wait()
    fill_mine(0, INWARD)
    pl.semaphore_wait(barrier, len(everyone))
    table.start()
    start(0, (FULL,))
    loads[1].wait()
    halve(1)
    start(1, (FULL,))
    loads[2].wait()
    halve(2)
    fill_mine(1, INWARD)
    start(0, INWARD)
    fill_mine(2, INWARD)
    for f in range(fields):
        fill_mine(f, (OWN,))
    for c in range(clusters):
        ob[c] = jnp.transpose(jnp.broadcast_to(onsite_ref[c : c + 1, :], (width, width)))

    loads[3].wait()
    loads[4].wait()
    inv_copy.wait()
    offsets = [3, 3 - s, 3 - 2 * s, 3 + 2 * s, 3 - 3 * s, 3 + s, 3 + 3 * s]

    def lay(c, _):
        for kind in range(7):
            for i in range(4):
                slot = 4 * offsets[kind] + i
                at = slice((4 * kind + i) * width, (4 * kind + i + 1) * width)
                kc[pl.ds(c * 256, width), at] = ks[inv_s[c, slot]]
                kc[pl.ds(c * 256 + width, width), at] = corr[inv_s[8 + c, slot]]
        return 0

    lax.fori_loop(0, clusters, lay, 0)
    start(1, INWARD)
    table.wait_recv()
    theirs_copy = pltpu.make_async_copy(theirs_v, theirs_s, table_sem.at[4])
    theirs_copy.start()
    theirs_copy.wait()
    energies = energies_ref[0:1, :]

    def fold(block):
        return jnp.sum(block.reshape(width // 8, 8, width), axis=0)

    def product(phases, a, b, wheres, fresh, thens=None):
        blocks = [gath[phase, 4 * a : 4 * b].reshape(4 * (b - a) * width, width) for phase in phases]
        block = blocks[0] if len(blocks) == 1 else jnp.concatenate(blocks, axis=1)

        def part(i, _):
            at = pl.ds(pl.multiple_of(i * 1024, 1024), 1024)
            wide = jnp.dot(kc[at, 4 * a * width : 4 * b * width], block, preferred_element_type=F32)
            for n, where in enumerate(wheres):
                out = wide[:, n * width : (n + 1) * width]
                if not fresh:
                    out = out + acc[where, at, :]
                if thens is None:
                    acc[where, at, :] = out
                else:
                    for j in range(4):
                        coupled = out[j * 256 : j * 256 + 128] - energies * out[j * 256 + 128 : j * 256 + 256]
                        thens[n](4 * i + j, coupled)
            return 0

        lax.fori_loop(0, 2, part, 0)

    def reduce_start(mine, got, stage):
        group = groups[stage]
        for distance, device in enumerate(group, 1):
            pltpu.make_async_remote_copy(
                src_ref=mine,
                dst_ref=got.at[len(group) - distance],
                send_sem=psend.at[stage],
                recv_sem=precv.at[stage],
                device_id=device,
                device_id_type=MESH,
            ).start()
        return pltpu.make_async_remote_copy(
            src_ref=got,
            dst_ref=got,
            send_sem=psend.at[stage],
            recv_sem=precv.at[stage],
            device_id=group[0],
            device_id_type=MESH,
        )

    def first_then_of(f):
        def first_then(c, coupled):
            r = r0[f][c]
            image = ob[c] * r + coupled
            y[f, c] = image
            vb[fields + f, c] = (r - STEP * image).astype(BF16)
            sums[f] += fold(r * r)
            sums[3 + f] += fold(r * image)
            sums[6 + f] += fold(image * image)

        return first_then

    def second_then_of(f):
        def second_then(c, coupled):
            r = r0[f][c]
            w = r - STEP * y[f, c]
            image = ob[c] * w + coupled
            z[f, c] = image
            sums[9 + f] += fold(w * image)
            sums[12 + f] += fold(r * image)

        return second_then

    def early(phases, wheres):
        for phase in phases:
            wait(phase, (SIB, IN2, IN3))
        product(phases, OWN, OUT1, wheres, True)

    def late(phases, wheres, thens):
        for phase in phases:
            wait(phase, (OUT1, OUT3))
        product(phases, OUT1, 7, wheres, False, thens)

    pass_on(0)
    start(2, (FULL,))
    early((0,), (0,))
    start(2, INWARD)
    pass_on(1)
    late((0,), (0,), (first_then_of(0),))
    start(3, (FULL,))
    fill_mine(3, INWARD)
    early((1,), (1,))
    start(3, INWARD)
    pass_on(2)
    late((1,), (1,), (first_then_of(1),))
    start(4, (FULL,))
    fill_mine(4, INWARD)
    early((2,), (2,))
    start(4, INWARD)
    late((2,), (2,), (first_then_of(2),))
    start(last, (FULL,))
    fill_mine(last, INWARD)
    start(last, INWARD)
    pass_on(3)
    for phase in range(fields, 2 * fields):
        fill_mine(phase, (OWN,))
    wait(last, (SIB,))
    product((last,), OWN, OUT2, (2,), True)
    pass_on(4)
    early((3, 4), (0, 1))
    pass_on(last)
    wait(last, (IN2, IN3))
    product((last,), OUT2, OUT1, (2,), False)
    late((3, 4), (0, 1), (second_then_of(0), second_then_of(1)))
    wait(last, (OUT1,))
    product((last,), OUT1, OUT3, (2,), False)
    corner = lax.broadcasted_iota(jnp.int32, (16, 128), 0) == lax.broadcasted_iota(jnp.int32, (16, 128), 1)
    column = jnp.sum(jnp.sum(sums[...], axis=1), axis=1, keepdims=True)
    part[...] = jnp.sum(jnp.where(corner, column, 0.0), axis=0, keepdims=True)
    wait(last, (OUT3,))
    product((last,), OUT3, 7, (2,), False, (second_then_of(2),))

    on_lane = lax.broadcasted_iota(jnp.int32, (1, 128), 1)
    for i in (11, 14):
        total = jnp.sum(jnp.sum(sums[i], axis=0, keepdims=True), axis=1, keepdims=True)
        part[...] = jnp.where(on_lane == i, total, part[...])
    stage_a = reduce_start(part, got, 0)
    for phase in copies:
        for copy in phase.values():
            copy.wait_send()
    table.wait_send()
    stage_a.wait_recv()
    partb[...] = part[...] + jnp.sum(got[...], axis=0)
    stage_b = reduce_start(partb, gotb, 1)
    stage_a.wait_send()
    stage_b.wait_recv()
    row_sums = partb[...] + jnp.sum(gotb[...], axis=0)
    whole = jnp.broadcast_to(row_sums, (8, 128))
    rr0, b0, yy, wz, rz = (whole if i == 0 else pltpu.roll(whole, 128 - 3 * i, 1) for i in range(5))
    alpha = rr0 / b0
    rr1 = rr0 + alpha * (alpha * yy - 2.0 * b0)
    gain = alpha / STEP
    keep = 1.0 - gain + rr1 / rr0
    bend = gain * gain * wz + gain * keep * (b0 - STEP * yy + rz) + keep * keep * b0
    step = rr1 / bend
    given = (alpha + step * (gain + keep), -step * gain * STEP, -(alpha + step * keep), -step * gain)
    for i, value in enumerate(given):
        for f in range(fields):
            coef_ref[3 * i + f : 3 * i + f + 1, :] = jnp.broadcast_to(value[0:1, f : f + 1], (1, 128))
    stage_b.wait_send()


def finish(r0a, r0b, r0c, y, z, coef_ref, x_hbm, res_hbm, x, res, out_sem):
    outs = []
    for f, r0 in enumerate((r0a, r0b, r0c)):
        a, b, c, d = (coef_ref[3 * i + f : 3 * i + f + 1, :] for i in range(4))
        for half in range(2):

            def one(i, _):
                i = 4 * half + i
                r, image = r0[i], y[f, i]
                x[f, i] = a * r + b * image
                res[f, i] = r + c * image + d * z[f, i]
                return 0

            lax.fori_loop(0, 4, one, 0)
            at = pl.ds(4 * half, 4)
            for array, out, which in ((x, x_hbm, 0), (res, res_hbm, 1)):
                outs.append(pltpu.make_async_copy(array.at[f, at], out.at[f, at], out_sem.at[which, f, half]))
                outs[-1].start()
    for out in outs:
        out.wait()


def body(right_side, onsite, energies, ks_tiles, correlation_tiles, tile_slot, readers):
    fields = right_side.shape[0]
    any_, vmem = pl.ANY, pltpu.VMEM
    spaces = (any_, vmem, vmem, any_, any_, vmem, vmem)
    field = (fields, 8, 128, 128)
    scratch = [
        pltpu.VMEM(field[1:], F32),
        pltpu.VMEM((6, 8, 128, 128), BF16),
        pltpu.VMEM((2048, 3584), BF16),
        pltpu.VMEM((193, 128, 128), BF16),
        pltpu.VMEM((65, 128, 128), BF16),
        pltpu.VMEM((3, 2048, 128), F32),
        pltpu.VMEM((6, 28, 128, 128), BF16),
        pltpu.VMEM((6, 7, 4, 128, 128), BF16),
        *[pltpu.VMEM((8, 128, 128), BF16) for _ in range(6)],
        pltpu.VMEM((16, 128), jnp.int32),
        pltpu.SMEM((16, 128), jnp.int32),
        pltpu.VMEM((8, 128), jnp.int32),
        pltpu.SMEM((8, 128), jnp.int32),
        pltpu.VMEM((8, 128), jnp.int32),
        pltpu.SMEM((8, 128), jnp.int32),
        pltpu.VMEM((16, 8, 128), F32),
        pltpu.VMEM((1, 128), F32),
        pltpu.VMEM((15, 1, 128), F32),
        pltpu.VMEM((1, 128), F32),
        pltpu.VMEM((15, 1, 128), F32),
        pltpu.SemaphoreType.DMA((5,)),
        pltpu.SemaphoreType.DMA((5,)),
        pltpu.SemaphoreType.DMA((6, 8)),
        pltpu.SemaphoreType.DMA((6, 8)),
        pltpu.SemaphoreType.DMA((2,)),
        pltpu.SemaphoreType.DMA((2,)),
    ]
    r0a, r0b, r0c, y, z, coef = pl.pallas_call(
        kernel,
        out_shape=(
            pltpu.VMEM(field[1:], F32),
            pltpu.VMEM(field[1:], F32),
            pltpu.VMEM(field[1:], F32),
            pltpu.VMEM(field, F32),
            pltpu.VMEM(field, F32),
            pltpu.VMEM((16, 128), F32),
        ),
        in_specs=[pl.BlockSpec(memory_space=s) for s in spaces],
        out_specs=(pl.BlockSpec(memory_space=vmem),) * 6,
        scratch_shapes=scratch,
        compiler_params=pltpu.CompilerParams(
            collective_id=0, has_side_effects=True, vmem_limit_bytes=59 << 20
        ),
    )(
        right_side.reshape(field),
        onsite.reshape(8, 128),
        energies.reshape(1, 128),
        ks_tiles.reshape(192, 128, 128),
        correlation_tiles.reshape(64, 128, 128),
        tile_slot,
        readers.reshape(7, 4).T,
    )
    x, res = pl.pallas_call(
        finish,
        out_shape=(jax.ShapeDtypeStruct(field, F32),) * 2,
        in_specs=[pl.BlockSpec(memory_space=s) for s in (vmem,) * 6],
        out_specs=(pl.BlockSpec(memory_space=any_),) * 2,
        scratch_shapes=[pltpu.VMEM(field, F32), pltpu.VMEM(field, F32), pltpu.SemaphoreType.DMA((2, 3, 2))],
        compiler_params=pltpu.CompilerParams(vmem_limit_bytes=24 << 20),
    )(r0a, r0b, r0c, y, z, coef)
    return x.reshape(right_side.shape), res.reshape(right_side.shape)


def solution(mesh):
    placed = (
        P(None, "row", "col"),
        P("row"),
        P("col"),
        P("row", None, None, None),
        P("row", None, None, None),
        P("row", None),
        P("row", None, None),
    )
    return jax.shard_map(
        body,
        mesh=mesh,
        in_specs=placed,
        out_specs=(P(None, "row", "col"), P(None, "row", "col")),
        check_vma=False,
    )
```

```python
import jax
import jax.numpy as jnp
from jax import lax
from jax.experimental import pallas as pl
from jax.experimental.pallas import tpu as pltpu
from jax.sharding import PartitionSpec as P

MESH = pl.DeviceIdType.MESH
F32 = jnp.float32
BF16 = jnp.bfloat16
SIZES = {"x": 4, "y": 4, "z": 8, "core": 2}
GROUPS = (("x", "y"), ("z", "core"))
STEP = 1.0 / 12.0
OWN, SIB, OUT2, IN2, IN3, OUT1, OUT3 = range(7)
FULL = 7


def members(axes, here):
    count, mine = 1, 0
    for a in axes:
        count *= SIZES[a]
        mine = mine * SIZES[a] + here[a]
    found = []
    for distance in range(1, count):
        there, rest = dict(here), lax.rem(mine + distance, count)
        for a in reversed(axes):
            there[a] = lax.rem(rest, SIZES[a])
            rest = rest // SIZES[a]
        found.append(((there["y"] * SIZES["z"] + there["z"]) * SIZES["core"] + there["core"], there["x"]))
    return found


def kernel(
    right_hbm, onsite_ref, energies_ref, ks_hbm, corr_hbm, slot_ref, readers_ref,
    r0a, r0b, r0c, y, z, coef_ref,
    ob, vb, kc, ks, corr, acc, gath, pack,
    full0, full1, full2, full3, full4, full5,
    inv_v, inv_s, mine_v, mine_s, theirs_v, theirs_s, sums,
    part, got, partb, gotb,
    load_sem, table_sem, send_sem, recv_sem, psend, precv,
):
    r0 = (r0a, r0b, r0c)
    full = (full0, full1, full2, full3, full4, full5)
    fields = len(r0)
    last = 2 * fields - 1
    clusters, width, slots = 8, 128, 28
    n_row = lax.axis_size("row")
    row, col = lax.axis_index("row"), lax.axis_index("col")
    core = lax.rem(row, 2)
    s = 2 * core - 1
    here = {"x": col, "y": row // 16, "z": lax.rem(row // 2, 8), "core": core}
    groups = [members(g, here) for g in GROUPS]

    def away(d):
        return (lax.rem(row + d + n_row, n_row), col)

    barrier = pltpu.get_barrier_semaphore()
    everyone = [away(d * s) for d in (-3, -2, -1, 1, 2)] + groups[0] + groups[1]
    for device in everyone:
        pl.semaphore_signal(barrier, 1, device_id=device, device_id_type=MESH)

    loads = [pltpu.make_async_copy(right_hbm.at[f], r0[f], load_sem.at[f]) for f in range(fields)]
    loads.append(pltpu.make_async_copy(ks_hbm, ks.at[pl.ds(0, 192)], load_sem.at[3]))
    loads.append(pltpu.make_async_copy(corr_hbm, corr.at[pl.ds(0, 64)], load_sem.at[4]))
    for load in loads:
        load.start()

    mine_v[...] = jnp.zeros_like(mine_v)
    mine_v[0:4, 0:7] = readers_ref[...]
    mine_copy = pltpu.make_async_copy(mine_v, mine_s, table_sem.at[0])
    mine_copy.start()

    lane = lax.broadcasted_iota(jnp.int32, (8, 128), 1)
    first = lax.broadcasted_iota(jnp.int32, (8, 128), 0)
    at_ks = jnp.full((8, 128), 192, jnp.int32)
    at_corr = jnp.full((8, 128), 64, jnp.int32)
    for k in range(24):
        hit = lane == slot_ref[:, k : k + 1]
        at_ks = jnp.where(hit, first * 24 + k, at_ks)
        if k < 8:
            at_corr = jnp.where(hit, first * 8 + k, at_corr)
    inv_v[0:8] = at_ks
    inv_v[8:16] = at_corr
    inv_copy = pltpu.make_async_copy(inv_v, inv_s, table_sem.at[1])
    inv_copy.start()
    ks[192] = jnp.zeros((width, width), BF16)
    corr[64] = jnp.zeros((width, width), BF16)
    sums[...] = jnp.zeros_like(sums)

    def remote(phase, kind, src, dst, d):
        return pltpu.make_async_remote_copy(
            src_ref=src,
            dst_ref=dst,
            send_sem=send_sem.at[phase, kind],
            recv_sem=recv_sem.at[phase, kind],
            device_id=away(d * s),
            device_id_type=MESH,
        )

    straight = {SIB: -1, IN2: -2, IN3: -3, OUT1: 1, OUT2: 2, OUT3: 3}
    hops = {SIB: -1, IN2: -2, IN3: -3, OUT1: -1, OUT3: 1}
    copies = []
    for phase in range(2 * fields):
        found = {
            kind: remote(phase, kind, pack.at[phase, kind], gath.at[phase, pl.ds(4 * kind, 4)], d)
            for kind, d in hops.items()
        }
        found[FULL] = remote(phase, FULL, vb.at[phase], full[phase], 2)
        copies.append(found)
    table = pltpu.make_async_remote_copy(
        src_ref=mine_v,
        dst_ref=theirs_v,
        send_sem=table_sem.at[2],
        recv_sem=table_sem.at[3],
        device_id=away(2 * s),
        device_id_type=MESH,
    )

    def fill(phase, kind, read, names, o):
        def one(i, _):
            block = read(names[i, o])
            if kind in (OWN, FULL):
                gath[phase, (4 * OWN if kind == OWN else 4 * OUT2) + i] = block
            else:
                pack[phase, kind, i] = block
            return 0

        lax.fori_loop(0, 4, one, 0)

    def fill_mine(phase, kinds):
        for kind in kinds:
            o = 3 if kind == OWN else 3 - straight[kind] * s
            fill(phase, kind, lambda c: vb[phase, c], mine_s, o)

    def start(phase, kinds):
        for kind in kinds:
            copies[phase][kind].start()

    def wait(phase, kinds):
        for kind in kinds:
            copies[phase][kind].wait_recv()

    INWARD = (IN3, IN2, SIB)

    def pass_on(phase):
        wait(phase, (FULL,))
        read = lambda c: full[phase][c]
        fill(phase, OUT3, read, theirs_s, 3 - 3 * s)
        start(phase, (OUT3,))
        fill(phase, OUT1, read, theirs_s, 3 - s)
        start(phase, (OUT1,))
        fill(phase, FULL, read, theirs_s, 3 - 2 * s)

    def halve(f):
        def one(c, _):
            vb[f, c] = r0[f][c].astype(BF16)
            return 0

        lax.fori_loop(0, clusters, one, 0)

    loads[0].wait()
    halve(0)
    mine_copy.wait()
    fill_mine(0, INWARD)
    pl.semaphore_wait(barrier, len(everyone))
    table.start()
    start(0, (FULL,))
    loads[1].wait()
    halve(1)
    start(1, (FULL,))
    loads[2].wait()
    halve(2)
    fill_mine(1, INWARD)
    start(0, INWARD)
    fill_mine(2, INWARD)
    for f in range(fields):
        fill_mine(f, (OWN,))
    for c in range(clusters):
        ob[c] = jnp.transpose(jnp.broadcast_to(onsite_ref[c : c + 1, :], (width, width)))

    loads[3].wait()
    loads[4].wait()
    inv_copy.wait()
    offsets = [3, 3 - s, 3 - 2 * s, 3 + 2 * s, 3 - 3 * s, 3 + s, 3 + 3 * s]

    def lay(c, _):
        for kind in range(7):
            for i in range(4):
                slot = 4 * offsets[kind] + i
                at = slice((4 * kind + i) * width, (4 * kind + i + 1) * width)
                kc[pl.ds(c * 256, width), at] = ks[inv_s[c, slot]]
                kc[pl.ds(c * 256 + width, width), at] = corr[inv_s[8 + c, slot]]
        return 0

    lax.fori_loop(0, clusters, lay, 0)
    start(1, INWARD)
    table.wait_recv()
    theirs_copy = pltpu.make_async_copy(theirs_v, theirs_s, table_sem.at[4])
    theirs_copy.start()
    theirs_copy.wait()
    energies = energies_ref[0:1, :]

    def fold(block):
        return jnp.sum(block.reshape(width // 8, 8, width), axis=0)

    def product(phases, a, b, wheres, fresh, thens=None):
        blocks = [gath[phase, 4 * a : 4 * b].reshape(4 * (b - a) * width, width) for phase in phases]
        block = blocks[0] if len(blocks) == 1 else jnp.concatenate(blocks, axis=1)

        def part(i, _):
            at = pl.ds(pl.multiple_of(i * 1024, 1024), 1024)
            wide = jnp.dot(kc[at, 4 * a * width : 4 * b * width], block, preferred_element_type=F32)
            for n, where in enumerate(wheres):
                out = wide[:, n * width : (n + 1) * width]
                if not fresh:
                    out = out + acc[where, at, :]
                if thens is None:
                    acc[where, at, :] = out
                else:
                    for j in range(4):
                        coupled = out[j * 256 : j * 256 + 128] - energies * out[j * 256 + 128 : j * 256 + 256]
                        thens[n](4 * i + j, coupled)
            return 0

        lax.fori_loop(0, 2, part, 0)

    def reduce_start(mine, got, stage):
        group = groups[stage]
        for distance, device in enumerate(group, 1):
            pltpu.make_async_remote_copy(
                src_ref=mine,
                dst_ref=got.at[len(group) - distance],
                send_sem=psend.at[stage],
                recv_sem=precv.at[stage],
                device_id=device,
                device_id_type=MESH,
            ).start()
        return pltpu.make_async_remote_copy(
            src_ref=got,
            dst_ref=got,
            send_sem=psend.at[stage],
            recv_sem=precv.at[stage],
            device_id=group[0],
            device_id_type=MESH,
        )

    def first_then_of(f):
        def first_then(c, coupled):
            r = r0[f][c]
            image = ob[c] * r + coupled
            y[f, c] = image
            vb[fields + f, c] = (r - STEP * image).astype(BF16)
            sums[f] += fold(r * r)
            sums[3 + f] += fold(r * image)
            sums[6 + f] += fold(image * image)

        return first_then

    def second_then_of(f):
        def second_then(c, coupled):
            r = r0[f][c]
            w = r - STEP * y[f, c]
            image = ob[c] * w + coupled
            z[f, c] = image
            sums[9 + f] += fold(w * image)
            sums[12 + f] += fold(r * image)

        return second_then

    def early(phases, wheres):
        for phase in phases:
            wait(phase, (SIB, IN2, IN3))
        product(phases, OWN, OUT1, wheres, True)

    def late(phases, wheres, thens):
        for phase in phases:
            wait(phase, (OUT1, OUT3))
        product(phases, OUT1, 7, wheres, False, thens)

    pass_on(0)
    start(2, (FULL,))
    start(2, INWARD)
    early((0,), (0,))
    pass_on(1)
    late((0,), (0,), (first_then_of(0),))
    start(3, (FULL,))
    fill_mine(3, INWARD)
    start(3, INWARD)
    early((1,), (1,))
    pass_on(2)
    late((1,), (1,), (first_then_of(1),))
    start(4, (FULL,))
    fill_mine(4, INWARD)
    start(4, INWARD)
    early((2,), (2,))
    late((2,), (2,), (first_then_of(2),))
    start(last, (FULL,))
    fill_mine(last, INWARD)
    start(last, INWARD)
    pass_on(3)
    for phase in range(fields, 2 * fields):
        fill_mine(phase, (OWN,))
    wait(last, (SIB,))
    product((last,), OWN, OUT2, (2,), True)
    pass_on(4)
    early((3, 4), (0, 1))
    pass_on(last)
    wait(last, (IN2, IN3))
    product((last,), OUT2, OUT1, (2,), False)
    wait(last, (OUT1,))
    product((last,), OUT1, OUT3, (2,), False)
    late((3, 4), (0, 1), (second_then_of(0), second_then_of(1)))
    corner = lax.broadcasted_iota(jnp.int32, (16, 128), 0) == lax.broadcasted_iota(jnp.int32, (16, 128), 1)
    column = jnp.sum(jnp.sum(sums[...], axis=1), axis=1, keepdims=True)
    part[...] = jnp.sum(jnp.where(corner, column, 0.0), axis=0, keepdims=True)
    wait(last, (OUT3,))
    product((last,), OUT3, 7, (2,), False, (second_then_of(2),))

    on_lane = lax.broadcasted_iota(jnp.int32, (1, 128), 1)
    for i in (11, 14):
        total = jnp.sum(jnp.sum(sums[i], axis=0, keepdims=True), axis=1, keepdims=True)
        part[...] = jnp.where(on_lane == i, total, part[...])
    stage_a = reduce_start(part, got, 0)
    for phase in copies:
        for copy in phase.values():
            copy.wait_send()
    table.wait_send()
    stage_a.wait_recv()
    partb[...] = part[...] + jnp.sum(got[...], axis=0)
    stage_b = reduce_start(partb, gotb, 1)
    stage_a.wait_send()
    stage_b.wait_recv()
    row_sums = partb[...] + jnp.sum(gotb[...], axis=0)
    whole = jnp.broadcast_to(row_sums, (8, 128))
    rr0, b0, yy, wz, rz = (whole if i == 0 else pltpu.roll(whole, 128 - 3 * i, 1) for i in range(5))
    alpha = rr0 / b0
    rr1 = rr0 + alpha * (alpha * yy - 2.0 * b0)
    gain = alpha / STEP
    keep = 1.0 - gain + rr1 / rr0
    bend = gain * gain * wz + gain * keep * (b0 - STEP * yy + rz) + keep * keep * b0
    step = rr1 / bend
    given = (alpha + step * (gain + keep), -step * gain * STEP, -(alpha + step * keep), -step * gain)
    for i, value in enumerate(given):
        for f in range(fields):
            coef_ref[3 * i + f : 3 * i + f + 1, :] = jnp.broadcast_to(value[0:1, f : f + 1], (1, 128))
    stage_b.wait_send()


def finish(r0a, r0b, r0c, y, z, coef_ref, x_hbm, res_hbm, x, res, out_sem):
    outs = []
    for f, r0 in enumerate((r0a, r0b, r0c)):
        a, b, c, d = (coef_ref[3 * i + f : 3 * i + f + 1, :] for i in range(4))
        for half in range(2):

            def one(i, _):
                i = 4 * half + i
                r, image = r0[i], y[f, i]
                x[f, i] = a * r + b * image
                res[f, i] = r + c * image + d * z[f, i]
                return 0

            lax.fori_loop(0, 4, one, 0)
            at = pl.ds(4 * half, 4)
            for array, out, which in ((x, x_hbm, 0), (res, res_hbm, 1)):
                outs.append(pltpu.make_async_copy(array.at[f, at], out.at[f, at], out_sem.at[which, f, half]))
                outs[-1].start()
    for out in outs:
        out.wait()


def body(right_side, onsite, energies, ks_tiles, correlation_tiles, tile_slot, readers):
    fields = right_side.shape[0]
    any_, vmem = pl.ANY, pltpu.VMEM
    spaces = (any_, vmem, vmem, any_, any_, vmem, vmem)
    field = (fields, 8, 128, 128)
    scratch = [
        pltpu.VMEM(field[1:], F32),
        pltpu.VMEM((6, 8, 128, 128), BF16),
        pltpu.VMEM((2048, 3584), BF16),
        pltpu.VMEM((193, 128, 128), BF16),
        pltpu.VMEM((65, 128, 128), BF16),
        pltpu.VMEM((3, 2048, 128), F32),
        pltpu.VMEM((6, 28, 128, 128), BF16),
        pltpu.VMEM((6, 7, 4, 128, 128), BF16),
        *[pltpu.VMEM((8, 128, 128), BF16) for _ in range(6)],
        pltpu.VMEM((16, 128), jnp.int32),
        pltpu.SMEM((16, 128), jnp.int32),
        pltpu.VMEM((8, 128), jnp.int32),
        pltpu.SMEM((8, 128), jnp.int32),
        pltpu.VMEM((8, 128), jnp.int32),
        pltpu.SMEM((8, 128), jnp.int32),
        pltpu.VMEM((16, 8, 128), F32),
        pltpu.VMEM((1, 128), F32),
        pltpu.VMEM((15, 1, 128), F32),
        pltpu.VMEM((1, 128), F32),
        pltpu.VMEM((15, 1, 128), F32),
        pltpu.SemaphoreType.DMA((5,)),
        pltpu.SemaphoreType.DMA((5,)),
        pltpu.SemaphoreType.DMA((6, 8)),
        pltpu.SemaphoreType.DMA((6, 8)),
        pltpu.SemaphoreType.DMA((2,)),
        pltpu.SemaphoreType.DMA((2,)),
    ]
    r0a, r0b, r0c, y, z, coef = pl.pallas_call(
        kernel,
        out_shape=(
            pltpu.VMEM(field[1:], F32),
            pltpu.VMEM(field[1:], F32),
            pltpu.VMEM(field[1:], F32),
            pltpu.VMEM(field, F32),
            pltpu.VMEM(field, F32),
            pltpu.VMEM((16, 128), F32),
        ),
        in_specs=[pl.BlockSpec(memory_space=s) for s in spaces],
        out_specs=(pl.BlockSpec(memory_space=vmem),) * 6,
        scratch_shapes=scratch,
        compiler_params=pltpu.CompilerParams(
            collective_id=0, has_side_effects=True, vmem_limit_bytes=59 << 20
        ),
    )(
        right_side.reshape(field),
        onsite.reshape(8, 128),
        energies.reshape(1, 128),
        ks_tiles.reshape(192, 128, 128),
        correlation_tiles.reshape(64, 128, 128),
        tile_slot,
        readers.reshape(7, 4).T,
    )
    x, res = pl.pallas_call(
        finish,
        out_shape=(jax.ShapeDtypeStruct(field, F32),) * 2,
        in_specs=[pl.BlockSpec(memory_space=s) for s in (vmem,) * 6],
        out_specs=(pl.BlockSpec(memory_space=any_),) * 2,
        scratch_shapes=[pltpu.VMEM(field, F32), pltpu.VMEM(field, F32), pltpu.SemaphoreType.DMA((2, 3, 2))],
        compiler_params=pltpu.CompilerParams(vmem_limit_bytes=24 << 20),
    )(r0a, r0b, r0c, y, z, coef)
    return x.reshape(right_side.shape), res.reshape(right_side.shape)


def solution(mesh):
    placed = (
        P(None, "row", "col"),
        P("row"),
        P("col"),
        P("row", None, None, None),
        P("row", None, None, None),
        P("row", None),
        P("row", None, None),
    )
    return jax.shard_map(
        body,
        mesh=mesh,
        in_specs=placed,
        out_specs=(P(None, "row", "col"), P(None, "row", "col")),
        check_vma=False,
    )
```

```python
import jax
import jax.numpy as jnp
from jax import lax
from jax.experimental import pallas as pl
from jax.experimental.pallas import tpu as pltpu
from jax.sharding import PartitionSpec as P

MESH = pl.DeviceIdType.MESH
F32 = jnp.float32
BF16 = jnp.bfloat16
SIZES = {"x": 4, "y": 4, "z": 8, "core": 2}
GROUPS = (("x", "y"), ("z", "core"))
STEP = 1.0 / 12.0
OWN, SIB, OUT2, IN2, IN3, OUT1, OUT3 = range(7)
FULL = 7


def members(axes, here):
    count, mine = 1, 0
    for a in axes:
        count *= SIZES[a]
        mine = mine * SIZES[a] + here[a]
    found = []
    for distance in range(1, count):
        there, rest = dict(here), lax.rem(mine + distance, count)
        for a in reversed(axes):
            there[a] = lax.rem(rest, SIZES[a])
            rest = rest // SIZES[a]
        found.append(((there["y"] * SIZES["z"] + there["z"]) * SIZES["core"] + there["core"], there["x"]))
    return found


def kernel(
    right_hbm, onsite_ref, energies_ref, ks_hbm, corr_hbm, slot_ref, readers_ref,
    r0a, r0b, r0c, y, z, coef_ref,
    ob, vb, kc, ks, corr, acc, gath, pack,
    full0, full1, full2, full3, full4, full5,
    inv_v, inv_s, mine_v, mine_s, theirs_v, theirs_s, sums,
    part, got, partb, gotb,
    load_sem, table_sem, send_sem, recv_sem, psend, precv,
):
    r0 = (r0a, r0b, r0c)
    full = (full0, full1, full2, full3, full4, full5)
    fields = len(r0)
    last = 2 * fields - 1
    clusters, width, slots = 8, 128, 28
    n_row = lax.axis_size("row")
    row, col = lax.axis_index("row"), lax.axis_index("col")
    core = lax.rem(row, 2)
    s = 2 * core - 1
    here = {"x": col, "y": row // 16, "z": lax.rem(row // 2, 8), "core": core}
    groups = [members(g, here) for g in GROUPS]

    def away(d):
        return (lax.rem(row + d + n_row, n_row), col)

    barrier = pltpu.get_barrier_semaphore()
    everyone = groups[0] + groups[1] + [away(d * s) for d in (-3, -2, -1, 1, 2)]
    for device in everyone:
        pl.semaphore_signal(barrier, 1, device_id=device, device_id_type=MESH)

    loads = [pltpu.make_async_copy(right_hbm.at[f], r0[f], load_sem.at[f]) for f in range(fields)]
    loads.append(pltpu.make_async_copy(ks_hbm, ks.at[pl.ds(0, 192)], load_sem.at[3]))
    loads.append(pltpu.make_async_copy(corr_hbm, corr.at[pl.ds(0, 64)], load_sem.at[4]))
    for load in loads:
        load.start()

    mine_v[...] = jnp.zeros_like(mine_v)
    mine_v[0:4, 0:7] = readers_ref[...]
    mine_copy = pltpu.make_async_copy(mine_v, mine_s, table_sem.at[0])
    mine_copy.start()

    lane = lax.broadcasted_iota(jnp.int32, (8, 128), 1)
    first = lax.broadcasted_iota(jnp.int32, (8, 128), 0)
    at_ks = jnp.full((8, 128), 192, jnp.int32)
    at_corr = jnp.full((8, 128), 64, jnp.int32)
    for k in range(24):
        hit = lane == slot_ref[:, k : k + 1]
        at_ks = jnp.where(hit, first * 24 + k, at_ks)
        if k < 8:
            at_corr = jnp.where(hit, first * 8 + k, at_corr)
    inv_v[0:8] = at_ks
    inv_v[8:16] = at_corr
    inv_copy = pltpu.make_async_copy(inv_v, inv_s, table_sem.at[1])
    inv_copy.start()
    ks[192] = jnp.zeros((width, width), BF16)
    corr[64] = jnp.zeros((width, width), BF16)
    sums[...] = jnp.zeros_like(sums)

    def remote(phase, kind, src, dst, d):
        return pltpu.make_async_remote_copy(
            src_ref=src,
            dst_ref=dst,
            send_sem=send_sem.at[phase, kind],
            recv_sem=recv_sem.at[phase, kind],
            device_id=away(d * s),
            device_id_type=MESH,
        )

    straight = {SIB: -1, IN2: -2, IN3: -3, OUT1: 1, OUT2: 2, OUT3: 3}
    hops = {SIB: -1, IN2: -2, IN3: -3, OUT1: -1, OUT3: 1}
    copies = []
    for phase in range(2 * fields):
        found = {
            kind: remote(phase, kind, pack.at[phase, kind], gath.at[phase, pl.ds(4 * kind, 4)], d)
            for kind, d in hops.items()
        }
        found[FULL] = remote(phase, FULL, vb.at[phase], full[phase], 2)
        copies.append(found)
    table = pltpu.make_async_remote_copy(
        src_ref=mine_v,
        dst_ref=theirs_v,
        send_sem=table_sem.at[2],
        recv_sem=table_sem.at[3],
        device_id=away(2 * s),
        device_id_type=MESH,
    )

    def fill(phase, kind, read, names, o):
        def one(i, _):
            block = read(names[i, o])
            if kind in (OWN, FULL):
                gath[phase, (4 * OWN if kind == OWN else 4 * OUT2) + i] = block
            else:
                pack[phase, kind, i] = block
            return 0

        lax.fori_loop(0, 4, one, 0)

    def fill_mine(phase, kinds):
        for kind in kinds:
            o = 3 if kind == OWN else 3 - straight[kind] * s
            fill(phase, kind, lambda c: vb[phase, c], mine_s, o)

    def start(phase, kinds):
        for kind in kinds:
            copies[phase][kind].start()

    def wait(phase, kinds):
        for kind in kinds:
            copies[phase][kind].wait_recv()

    INWARD = (IN3, IN2, SIB)

    def pass_on(phase):
        wait(phase, (FULL,))
        read = lambda c: full[phase][c]
        fill(phase, OUT3, read, theirs_s, 3 - 3 * s)
        start(phase, (OUT3,))
        fill(phase, OUT1, read, theirs_s, 3 - s)
        start(phase, (OUT1,))
        fill(phase, FULL, read, theirs_s, 3 - 2 * s)

    def halve(f):
        def one(c, _):
            vb[f, c] = r0[f][c].astype(BF16)
            return 0

        lax.fori_loop(0, clusters, one, 0)

    loads[0].wait()
    halve(0)
    mine_copy.wait()
    fill_mine(0, INWARD)
    pl.semaphore_wait(barrier, len(everyone))
    table.start()
    start(0, (FULL,))
    loads[1].wait()
    halve(1)
    start(1, (FULL,))
    loads[2].wait()
    halve(2)
    fill_mine(1, INWARD)
    start(0, INWARD)
    fill_mine(2, INWARD)
    for f in range(fields):
        fill_mine(f, (OWN,))
    for c in range(clusters):
        ob[c] = jnp.transpose(jnp.broadcast_to(onsite_ref[c : c + 1, :], (width, width)))

    loads[3].wait()
    loads[4].wait()
    inv_copy.wait()
    offsets = [3, 3 - s, 3 - 2 * s, 3 + 2 * s, 3 - 3 * s, 3 + s, 3 + 3 * s]

    def lay(c, _):
        for kind in range(7):
            for i in range(4):
                slot = 4 * offsets[kind] + i
                at = slice((4 * kind + i) * width, (4 * kind + i + 1) * width)
                kc[pl.ds(c * 256, width), at] = ks[inv_s[c, slot]]
                kc[pl.ds(c * 256 + width, width), at] = corr[inv_s[8 + c, slot]]
        return 0

    lax.fori_loop(0, clusters, lay, 0)
    start(1, INWARD)
    table.wait_recv()
    theirs_copy = pltpu.make_async_copy(theirs_v, theirs_s, table_sem.at[4])
    theirs_copy.start()
    theirs_copy.wait()
    energies = energies_ref[0:1, :]

    def fold(block):
        return jnp.sum(block.reshape(width // 8, 8, width), axis=0)

    def product(phases, a, b, wheres, fresh, thens=None):
        blocks = [gath[phase, 4 * a : 4 * b].reshape(4 * (b - a) * width, width) for phase in phases]
        block = blocks[0] if len(blocks) == 1 else jnp.concatenate(blocks, axis=1)

        def part(i, _):
            at = pl.ds(pl.multiple_of(i * 1024, 1024), 1024)
            wide = jnp.dot(kc[at, 4 * a * width : 4 * b * width], block, preferred_element_type=F32)
            for n, where in enumerate(wheres):
                out = wide[:, n * width : (n + 1) * width]
                if not fresh:
                    out = out + acc[where, at, :]
                if thens is None:
                    acc[where, at, :] = out
                else:
                    for j in range(4):
                        coupled = out[j * 256 : j * 256 + 128] - energies * out[j * 256 + 128 : j * 256 + 256]
                        thens[n](4 * i + j, coupled)
            return 0

        lax.fori_loop(0, 2, part, 0)

    def reduce_start(mine, got, stage):
        group = groups[stage]
        inner = SIZES[GROUPS[stage][1]]
        outer = SIZES[GROUPS[stage][0]]
        far = lambda d: -min(d // inner, outer - d // inner) - min(d % inner, inner - d % inner)
        for distance in sorted(range(1, len(group) + 1), key=far):
            device = group[distance - 1]
            pltpu.make_async_remote_copy(
                src_ref=mine,
                dst_ref=got.at[len(group) - distance],
                send_sem=psend.at[stage],
                recv_sem=precv.at[stage],
                device_id=device,
                device_id_type=MESH,
            ).start()
        return pltpu.make_async_remote_copy(
            src_ref=got,
            dst_ref=got,
            send_sem=psend.at[stage],
            recv_sem=precv.at[stage],
            device_id=group[0],
            device_id_type=MESH,
        )

    def first_then_of(f):
        def first_then(c, coupled):
            r = r0[f][c]
            image = ob[c] * r + coupled
            y[f, c] = image
            vb[fields + f, c] = (r - STEP * image).astype(BF16)
            sums[f] += fold(r * r)
            sums[3 + f] += fold(r * image)
            sums[6 + f] += fold(image * image)

        return first_then

    def second_then_of(f):
        def second_then(c, coupled):
            r = r0[f][c]
            w = r - STEP * y[f, c]
            image = ob[c] * w + coupled
            z[f, c] = image
            sums[9 + f] += fold(w * image)
            sums[12 + f] += fold(r * image)

        return second_then

    def early(phases, wheres):
        for phase in phases:
            wait(phase, (SIB, IN2, IN3))
        product(phases, OWN, OUT1, wheres, True)

    def late(phases, wheres, thens):
        for phase in phases:
            wait(phase, (OUT1, OUT3))
        product(phases, OUT1, 7, wheres, False, thens)

    pass_on(0)
    start(2, (FULL,))
    start(2, INWARD)
    early((0,), (0,))
    pass_on(1)
    late((0,), (0,), (first_then_of(0),))
    start(3, (FULL,))
    fill_mine(3, INWARD)
    start(3, INWARD)
    early((1,), (1,))
    pass_on(2)
    late((1,), (1,), (first_then_of(1),))
    start(4, (FULL,))
    fill_mine(4, INWARD)
    start(4, INWARD)
    early((2,), (2,))
    late((2,), (2,), (first_then_of(2),))
    start(last, (FULL,))
    fill_mine(last, INWARD)
    start(last, INWARD)
    pass_on(3)
    for phase in range(fields, 2 * fields):
        fill_mine(phase, (OWN,))
    wait(last, (SIB,))
    product((last,), OWN, OUT2, (2,), True)
    pass_on(4)
    early((3, 4), (0, 1))
    pass_on(last)
    wait(last, (IN2, IN3))
    product((last,), OUT2, OUT1, (2,), False)
    wait(last, (OUT1,))
    product((last,), OUT1, OUT3, (2,), False)
    late((3, 4), (0, 1), (second_then_of(0), second_then_of(1)))
    corner = lax.broadcasted_iota(jnp.int32, (16, 128), 0) == lax.broadcasted_iota(jnp.int32, (16, 128), 1)
    column = jnp.sum(jnp.sum(sums[...], axis=1), axis=1, keepdims=True)
    part[...] = jnp.sum(jnp.where(corner, column, 0.0), axis=0, keepdims=True)
    wait(last, (OUT3,))
    product((last,), OUT3, 7, (2,), False, (second_then_of(2),))

    on_lane = lax.broadcasted_iota(jnp.int32, (1, 128), 1)
    for i in (11, 14):
        total = jnp.sum(jnp.sum(sums[i], axis=0, keepdims=True), axis=1, keepdims=True)
        part[...] = jnp.where(on_lane == i, total, part[...])
    stage_a = reduce_start(part, got, 0)
    for phase in copies:
        for copy in phase.values():
            copy.wait_send()
    table.wait_send()
    stage_a.wait_recv()
    partb[...] = part[...] + jnp.sum(got[...], axis=0)
    stage_b = reduce_start(partb, gotb, 1)
    stage_a.wait_send()
    stage_b.wait_recv()
    row_sums = partb[...] + jnp.sum(gotb[...], axis=0)
    whole = jnp.broadcast_to(row_sums, (8, 128))
    rr0, b0, yy, wz, rz = (whole if i == 0 else pltpu.roll(whole, 128 - 3 * i, 1) for i in range(5))
    alpha = rr0 / b0
    rr1 = rr0 + alpha * (alpha * yy - 2.0 * b0)
    gain = alpha / STEP
    keep = 1.0 - gain + rr1 / rr0
    bend = gain * gain * wz + gain * keep * (b0 - STEP * yy + rz) + keep * keep * b0
    step = rr1 / bend
    given = (alpha + step * (gain + keep), -step * gain * STEP, -(alpha + step * keep), -step * gain)
    for i, value in enumerate(given):
        for f in range(fields):
            coef_ref[3 * i + f : 3 * i + f + 1, :] = jnp.broadcast_to(value[0:1, f : f + 1], (1, 128))
    stage_b.wait_send()


def finish(r0a, r0b, r0c, y, z, coef_ref, x_hbm, res_hbm, x, res, out_sem):
    outs = []
    for f, r0 in enumerate((r0a, r0b, r0c)):
        a, b, c, d = (coef_ref[3 * i + f : 3 * i + f + 1, :] for i in range(4))
        for half in range(2):

            def one(i, _):
                i = 4 * half + i
                r, image = r0[i], y[f, i]
                x[f, i] = a * r + b * image
                res[f, i] = r + c * image + d * z[f, i]
                return 0

            lax.fori_loop(0, 4, one, 0)
            at = pl.ds(4 * half, 4)
            for array, out, which in ((x, x_hbm, 0), (res, res_hbm, 1)):
                outs.append(pltpu.make_async_copy(array.at[f, at], out.at[f, at], out_sem.at[which, f, half]))
                outs[-1].start()
    for out in outs:
        out.wait()


def body(right_side, onsite, energies, ks_tiles, correlation_tiles, tile_slot, readers):
    fields = right_side.shape[0]
    any_, vmem = pl.ANY, pltpu.VMEM
    spaces = (any_, vmem, vmem, any_, any_, vmem, vmem)
    field = (fields, 8, 128, 128)
    scratch = [
        pltpu.VMEM(field[1:], F32),
        pltpu.VMEM((6, 8, 128, 128), BF16),
        pltpu.VMEM((2048, 3584), BF16),
        pltpu.VMEM((193, 128, 128), BF16),
        pltpu.VMEM((65, 128, 128), BF16),
        pltpu.VMEM((3, 2048, 128), F32),
        pltpu.VMEM((6, 28, 128, 128), BF16),
        pltpu.VMEM((6, 7, 4, 128, 128), BF16),
        *[pltpu.VMEM((8, 128, 128), BF16) for _ in range(6)],
        pltpu.VMEM((16, 128), jnp.int32),
        pltpu.SMEM((16, 128), jnp.int32),
        pltpu.VMEM((8, 128), jnp.int32),
        pltpu.SMEM((8, 128), jnp.int32),
        pltpu.VMEM((8, 128), jnp.int32),
        pltpu.SMEM((8, 128), jnp.int32),
        pltpu.VMEM((16, 8, 128), F32),
        pltpu.VMEM((1, 128), F32),
        pltpu.VMEM((15, 1, 128), F32),
        pltpu.VMEM((1, 128), F32),
        pltpu.VMEM((15, 1, 128), F32),
        pltpu.SemaphoreType.DMA((5,)),
        pltpu.SemaphoreType.DMA((5,)),
        pltpu.SemaphoreType.DMA((6, 8)),
        pltpu.SemaphoreType.DMA((6, 8)),
        pltpu.SemaphoreType.DMA((2,)),
        pltpu.SemaphoreType.DMA((2,)),
    ]
    r0a, r0b, r0c, y, z, coef = pl.pallas_call(
        kernel,
        out_shape=(
            pltpu.VMEM(field[1:], F32),
            pltpu.VMEM(field[1:], F32),
            pltpu.VMEM(field[1:], F32),
            pltpu.VMEM(field, F32),
            pltpu.VMEM(field, F32),
            pltpu.VMEM((16, 128), F32),
        ),
        in_specs=[pl.BlockSpec(memory_space=s) for s in spaces],
        out_specs=(pl.BlockSpec(memory_space=vmem),) * 6,
        scratch_shapes=scratch,
        compiler_params=pltpu.CompilerParams(
            collective_id=0, has_side_effects=True, vmem_limit_bytes=59 << 20
        ),
    )(
        right_side.reshape(field),
        onsite.reshape(8, 128),
        energies.reshape(1, 128),
        ks_tiles.reshape(192, 128, 128),
        correlation_tiles.reshape(64, 128, 128),
        tile_slot,
        readers.reshape(7, 4).T,
    )
    x, res = pl.pallas_call(
        finish,
        out_shape=(jax.ShapeDtypeStruct(field, F32),) * 2,
        in_specs=[pl.BlockSpec(memory_space=s) for s in (vmem,) * 6],
        out_specs=(pl.BlockSpec(memory_space=any_),) * 2,
        scratch_shapes=[pltpu.VMEM(field, F32), pltpu.VMEM(field, F32), pltpu.SemaphoreType.DMA((2, 3, 2))],
        compiler_params=pltpu.CompilerParams(vmem_limit_bytes=24 << 20),
    )(r0a, r0b, r0c, y, z, coef)
    return x.reshape(right_side.shape), res.reshape(right_side.shape)


def solution(mesh):
    placed = (
        P(None, "row", "col"),
        P("row"),
        P("col"),
        P("row", None, None, None),
        P("row", None, None, None),
        P("row", None),
        P("row", None, None),
    )
    return jax.shard_map(
        body,
        mesh=mesh,
        in_specs=placed,
        out_specs=(P(None, "row", "col"), P(None, "row", "col")),
        check_vma=False,
    )
```
